32 devices in a mesh: row: 4 (over y, x), col: 8 (over z, core).
Axes of the slice: x: 2, y: 2, z: 4, core: 2. Of those that a mesh axis runs over, the one named last changes fastest.
Arguments:
- density: float32 [6144, 6144], P('row', 'col'), may hold values from -1 to 1, as said below
- response: float32 [6144, 6144], P('row', 'col'), may hold values from -1 to 1, as said below
- density_mask: int32 [48, 48], replicated, may hold values from 0 to 1, as said below
- response_mask: int32 [48, 48], replicated, may hold values from 0 to 1, as said below
- branch: int32 [48], replicated, may hold values from 0 to 1
Outputs:
- new_density: float32 [6144, 6144], P('row', 'col')
- new_response: float32 [6144, 6144], P('row', 'col')
The draws below stay inside these ranges and needn't reach their ends.
Inputs may be any that keep to these rules, and one draw needn't show every extreme that they name: `density`: symmetric: equal to its own transpose. `response`: symmetric: equal to its own transpose. `density_mask`: symmetric, with ones on the diagonal. `response_mask`: symmetric, with ones on the diagonal.
All inputs are finite; a program needn't handle non-finite values.
Results may differ from the reference program's by a relative error of at most 0.000067.
Values sent between devices are 32-bit elements; how exact they have to be, the bound alone decides.
A program may use at most 192 MiB of HBM per device.

```python
import math
import jax
import jax.numpy as jnp
from jax import lax

N = 6144
BLOCK = 128
NB = 48


def pattern(key):
    coins = jax.random.randint(key, (NB, NB), 0, 2, jnp.int32)
    row_ids = lax.broadcasted_iota(jnp.int32, (NB, NB), 0)
    col_ids = lax.broadcasted_iota(jnp.int32, (NB, NB), 1)
    coins = jnp.where(row_ids <= col_ids, coins, coins.T)
    return jnp.where(row_ids == col_ids, 1, coins).astype(jnp.int32)


def draw_density_mask(key, part):
    return pattern(jax.random.fold_in(key, 11))


def draw_response_mask(key, part):
    return pattern(jax.random.fold_in(key, 12))


def draw_density(key, part):
    first_key = jax.random.fold_in(jax.random.fold_in(key, 21), 0)
    gauss = jax.random.normal(first_key, (N, N), jnp.float32)
    factor = (N / 2.0) ** (-0.25)
    return jnp.clip((gauss + gauss.T) * (factor * math.sqrt(0.5)), -1.0, 1.0)


def draw_response(key, part):
    first_key = jax.random.fold_in(jax.random.fold_in(key, 22), 0)
    gauss = jax.random.normal(first_key, (N, N), jnp.float32)
    factor = (N / 2.0) ** (-0.25)
    return jnp.clip((gauss + gauss.T) * (factor * math.sqrt(0.5)), -1.0, 1.0)


def touch_ends(drawn, key, smallest, top_value):
    place = [jax.random.randint(jax.random.fold_in(key, axis), (), 0, length) for axis, length in enumerate(drawn.shape)]
    main_axis = drawn.shape.index(max(drawn.shape))
    beside = place[:main_axis] + [(place[main_axis] + 1) % drawn.shape[main_axis]] + place[main_axis + 1:]
    return drawn.at[tuple(place)].set(smallest).at[tuple(beside)].set(top_value)


def setup_inputs(seed: int = 0) -> dict:
    splits = jax.random.split(jax.random.key(seed), 6)
    return {
        "density": draw_density(jax.random.fold_in(splits[5], 71), 0),
        "response": draw_response(jax.random.fold_in(splits[5], 71), 0),
        "density_mask": draw_density_mask(jax.random.fold_in(splits[5], 71), 0),
        "response_mask": draw_response_mask(jax.random.fold_in(splits[5], 71), 0),
        "branch": touch_ends(jax.random.randint(splits[4], (NB,), 0, 2), jax.random.fold_in(splits[4], 1), 0, 1).astype(jnp.int32),
    }


def expand_mask(block_mask):
    return jnp.repeat(jnp.repeat(block_mask, BLOCK, 0), BLOCK, 1).astype(jnp.float32)


def reference(density, response, density_mask, response_mask, branch):
    masked_density = density * expand_mask(density_mask)
    masked_response = response * expand_mask(response_mask)
    square = jnp.dot(masked_density, masked_density, precision=lax.Precision.HIGHEST, preferred_element_type=jnp.float32)
    product = jnp.dot(masked_density, masked_response, precision=lax.Precision.HIGHEST, preferred_element_type=jnp.float32)
    combined = product + product.T
    chosen = jnp.repeat(branch, BLOCK)[:, None]
    new_density = jnp.where(chosen == 0, square, 2.0 * masked_density - square)
    new_response = jnp.where(chosen == 0, combined, 2.0 * masked_response - combined)
    return new_density, new_response
```

```python
import functools

import jax
import jax.numpy as jnp
from jax import lax
from jax.experimental import pallas as pl
from jax.experimental.pallas import tpu as pltpu
from jax.sharding import PartitionSpec as P

BLOCK = 128
CORES = 2
SHARES = ((5, 8), (3, 4))
VMEM = 60 * 2**20


precise = lax.Precision.HIGH


def expand_mask(local_tile, block_mask):
    row_count, col_count = local_tile.shape
    row_blocks = row_count // BLOCK
    col_blocks = col_count // BLOCK
    row_start = lax.axis_index("row") * row_blocks
    col_start = lax.axis_index("col") * col_blocks
    window = lax.dynamic_slice(block_mask, (row_start, col_start), (row_blocks, col_blocks)).astype(
        jnp.float32
    )
    shaped = local_tile.reshape(row_blocks, BLOCK, col_blocks, BLOCK) * window[:, None, :, None]
    return shaped.reshape(row_count, col_count)


def matmul(left, right):
    return jnp.dot(left, right, precision=precise, preferred_element_type=jnp.float32)


def whole_products(masked_density, masked_response):
    column_density, column_response = (
        lax.all_gather(masked_density, "row", axis=0, tiled=True),
        lax.all_gather(masked_response, "row", axis=0, tiled=True),
    )
    segments = (
        lax.all_gather(masked_density, "col", axis=1, tiled=True),
        lax.all_gather(masked_response, "col", axis=1, tiled=True),
    )
    square = matmul(segments[0], column_density)
    product = matmul(segments[0], column_response)
    reversed_tile = matmul(segments[1], column_density)
    return square, product + reversed_tile


def pack_kernel(row_blocks, col_blocks, slots, density, response, packed):
    for m, tile in enumerate((density, response)):

        @pl.loop(0, row_blocks)
        def _(i):
            rows = pl.ds(pl.multiple_of(i * BLOCK, BLOCK), BLOCK)
            for j in range(col_blocks):
                slot = slots[(m * row_blocks + i) * col_blocks + j]

                @pl.when(slot >= 0)
                def _():
                    packed[slot] = tile[rows, j * BLOCK : (j + 1) * BLOCK]


def pack(slots, density, response, capacity):
    rows, cols = density.shape
    return pl.pallas_call(
        functools.partial(pack_kernel, rows // BLOCK, cols // BLOCK),
        grid_spec=pltpu.PrefetchScalarGridSpec(
            num_scalar_prefetch=1,
            grid=(1,),
            in_specs=[pl.BlockSpec((rows, cols), lambda g, s: (0, 0))] * 2,
            out_specs=pl.BlockSpec((capacity, BLOCK, BLOCK), lambda g, s: (0, 0, 0)),
        ),
        out_shape=jax.ShapeDtypeStruct((capacity, BLOCK, BLOCK), jnp.float32),
        compiler_params=pltpu.CompilerParams(vmem_limit_bytes=VMEM),
        name="pack_blocks",
    )(slots, density, response)


def split(value):
    high = value.astype(jnp.bfloat16)
    return high, (value - high.astype(jnp.float32)).astype(jnp.bfloat16)


def accumulate_kernel(lhs, first, row_blocks, col_blocks, step_blocks, table, *refs):
    bufs, columns, refs = refs[:2], refs[2:4], refs[4:]
    before, refs = ((), refs) if first else (refs[:lhs], refs[lhs:])
    after, (left_high, left_low, right_high, right_low) = refs[:lhs], refs[lhs:]
    step = pl.program_id(0)
    depth = col_blocks * BLOCK
    width = right_high.shape[1]

    @pl.when(step == 0)
    def _():
        for b in range(2):

            @pl.loop(0, col_blocks)
            def _(i):
                source = pl.ds(pl.multiple_of(i * BLOCK, BLOCK), BLOCK)
                target = pl.ds(pl.multiple_of(b * depth + i * BLOCK, BLOCK), BLOCK)
                right_high[target, :], right_low[target, :] = split(columns[b][source, :])

    for b in range(2):
        for m in range(lhs):

            @pl.loop(0, step_blocks)
            def _(i):
                rows = pl.ds(pl.multiple_of(i * BLOCK, BLOCK), BLOCK)
                base = ((b * 2 + m) * row_blocks + step * step_blocks + i) * col_blocks
                for j in range(col_blocks):
                    slot = table[2 + base + j]
                    cols = slice(b * depth + j * BLOCK, b * depth + (j + 1) * BLOCK)

                    @pl.when(slot >= 0)
                    def _():
                        left_high[m, rows, cols], left_low[m, rows, cols] = split(bufs[b][slot])

                    @pl.when(slot < 0)
                    def _():
                        empty = jnp.zeros((BLOCK, BLOCK), jnp.bfloat16)
                        left_high[m, rows, cols] = empty
                        left_low[m, rows, cols] = empty

    tile = 2 * BLOCK if width % (2 * BLOCK) == 0 else BLOCK
    dot = functools.partial(jnp.dot, preferred_element_type=jnp.float32)
    for m in range(lhs):

        @pl.loop(0, width // tile)
        def _(t):
            cols = pl.ds(pl.multiple_of(t * tile, tile), tile)
            high, low = right_high[:, cols], right_low[:, cols]
            total = dot(left_high[m], high) + (dot(left_high[m], low) + dot(left_low[m], high))
            after[m][:, cols] = total if first else before[m][:, cols] + total


def accumulate(table, bufs, column, shape, lhs, before=None):
    rows, cols = shape
    row_blocks, col_blocks = rows // BLOCK, cols // BLOCK
    steps = 3 if row_blocks % 3 == 0 else 1
    step_rows = rows // steps
    first = before is None
    once = pl.Buffered(1)
    part = pl.BlockSpec((step_rows, cols), lambda g, s: (g, 0))
    capacity = bufs[0].shape[0]
    return pl.pallas_call(
        functools.partial(accumulate_kernel, lhs, first, row_blocks, col_blocks, row_blocks // steps),
        grid_spec=pltpu.PrefetchScalarGridSpec(
            num_scalar_prefetch=1,
            grid=(steps,),
            in_specs=[
                pl.BlockSpec((capacity, BLOCK, BLOCK), lambda g, s: (0, 0, 0), pipeline_mode=once)
            ]
            * 2
            + [
                pl.BlockSpec((cols, cols), lambda g, s: (s[0], 0), pipeline_mode=once),
                pl.BlockSpec((cols, cols), lambda g, s: (s[1], 0), pipeline_mode=once),
            ]
            + ([] if first else [part] * lhs),
            out_specs=[part] * lhs,
            scratch_shapes=[pltpu.VMEM((lhs, step_rows, 2 * cols), jnp.bfloat16)] * 2
            + [pltpu.VMEM((2 * cols, cols), jnp.bfloat16)] * 2,
        ),
        out_shape=[jax.ShapeDtypeStruct(shape, jnp.float32)] * lhs,
        input_output_aliases={} if first else {5 + m: m for m in range(lhs)},
        compiler_params=pltpu.CompilerParams(vmem_limit_bytes=VMEM),
        cost_estimate=pl.CostEstimate(
            flops=2 * 3 * lhs * rows * 2 * cols * cols,
            bytes_accessed=4 * (2 * cols * cols + 2 * lhs * rows * cols) + 8 * capacity * BLOCK * BLOCK,
            transcendentals=0,
        ),
        name="accumulate_blocks",
    )(table, *bufs, column, column, *(() if first else before))


def packed_products(capacity, density, response, masked_density, masked_response, slots):
    shape = density.shape
    devices = lax.axis_size("col")
    chips = devices // CORES
    order = [0] + list(range(1, chips, 2)) + list(range(2, chips, 2))[::-1]
    place = [order.index(z) for z in range(chips)]
    me = lax.axis_index("col")
    core = lax.rem(me, CORES)
    position = jnp.array(place, jnp.int32)[me // CORES]

    def move(value, by):
        pairs = [
            (order[p] * CORES + k, order[(p + by) % chips] * CORES + k)
            for p in range(chips)
            for k in range(CORES)
        ]
        return lax.ppermute(value, "col", pairs)

    def swap(value):
        return lax.ppermute(value, "col", [(d, d ^ 1) for d in range(devices)])

    column_density = lax.all_gather(masked_density, "row", axis=0, tiled=True)
    column_response = lax.all_gather(masked_response, "row", axis=0, tiled=True)

    mine = lax.dynamic_index_in_dim(slots, me, 0, keepdims=False)
    own = pack(mine, density, response, capacity)
    def paired(value, offset):
        chip = jnp.array(order, jnp.int32)[lax.rem(position + offset + chips, chips)]
        ids = [chip * CORES + core, chip * CORES + 1 - core]
        tables = [lax.dynamic_index_in_dim(slots, i, 0, keepdims=False) for i in ids]
        return jnp.concatenate([jnp.stack(ids), *tables]), (value, swap(value))

    pairs = [paired(own, 0)]
    ahead = behind = own
    for step in range(1, (chips + 1) // 2):
        ahead, behind = move(ahead, 1), move(behind, -1)
        pairs += [paired(ahead, -step), paired(behind, step)]
    last = ()
    if chips % 2 == 0:
        half = capacity // 2
        last = (move(ahead[:half], 1), move(behind[half:], -1))

    total = None
    for table, bufs in pairs:
        total = accumulate(table, bufs, column_density, shape, 2, total)
    if last:
        last, total = lax.optimization_barrier((last, total))
        pairs.append(paired(jnp.concatenate(last), chips // 2))
        total = accumulate(*pairs[-1], column_density, shape, 2, total)
    square, combined = total
    for table, bufs in pairs:
        (combined,) = accumulate(table, bufs, column_response, shape, 1, [combined])
    return square, combined


def per_device(density, response, density_mask, response_mask, branch):
    masked_density = expand_mask(density, density_mask)
    masked_response = expand_mask(response, response_mask)

    rows, cols = lax.axis_size("row"), lax.axis_size("col")
    row_blocks, col_blocks = density.shape[0] // BLOCK, density.shape[1] // BLOCK
    occupied = jnp.stack([density_mask, response_mask]).reshape(2, rows, row_blocks, cols, col_blocks)
    occupied = occupied.transpose(1, 3, 0, 2, 4).reshape(rows, cols, -1)
    fullest = jnp.max(jnp.sum(occupied, axis=-1))
    line = lax.dynamic_index_in_dim(occupied, lax.axis_index("row"), 0, keepdims=False)
    slots = jnp.where(line > 0, jnp.cumsum(line, axis=-1) - 1, -1).astype(jnp.int32)

    blocks = occupied.shape[-1]
    capacities = [blocks * share[0] // share[1] // 2 * 2 for share in SHARES]
    level = sum((fullest > capacity).astype(jnp.int32) for capacity in capacities)
    square, combined = lax.switch(
        level,
        [functools.partial(packed_products, capacity) for capacity in capacities]
        + [lambda d, r, md, mr, s: whole_products(md, mr)],
        density,
        response,
        masked_density,
        masked_response,
        slots,
    )

    local_blocks = density.shape[0] // BLOCK
    block_start = lax.axis_index("row") * local_blocks
    local_branch = lax.dynamic_slice_in_dim(branch, block_start, local_blocks, 0)
    chosen = jnp.repeat(local_branch, BLOCK)[:, None]
    new_density = jnp.where(chosen == 0, square, 2.0 * masked_density - square)
    new_response = jnp.where(chosen == 0, combined, 2.0 * masked_response - combined)
    return (new_density, new_response)


def solution(mesh):
    return jax.shard_map(
        per_device,
        mesh=mesh,
        in_specs=(P("row", "col"), P("row", "col"), P(), P(), P()),
        out_specs=(P("row", "col"), P("row", "col")),
        check_vma=False,
    )
```
